256 devices in a mesh: sx: 32 (over x_lo, z, core), sy: 8 (over y, x_hi).
Axes of the slice: x: 4 (x_hi: 2, x_lo: 2; x = x_hi * 2 + x_lo), y: 4, z: 8, core: 2. Of those that a mesh axis runs over, the one named last changes fastest.
Arguments:
- field: float32 [2, 16, 128, 64, 1024], P(None, None, 'sx', 'sy'), may hold values from -6 to 6
- grad_out: float32 [2, 16, 128, 64, 1024], P(None, None, 'sx', 'sy'), may hold values from -6 to 6
- local_weight: float32 [16, 16], replicated, may hold values from -1.5 to 1.5
- mode_weight: float32 [2, 16, 16, 32768], P(None, None, None, ('sx', 'sy')), may hold values from -1 to 1
- mode_x: int32 [16], replicated, may hold values from 0 to 127, as said below
- mode_y: int32 [16], replicated, may hold values from 0 to 63, as said below
- mode_z: int32 [16], replicated, may hold values from 0 to 63, as said below
- mode_t: int32 [8], replicated, may hold values from 0 to 15, as said below
Outputs:
- grad_input: float32 [2, 16, 128, 64, 1024], P(None, None, 'sx', 'sy')
- grad_modes: float32 [2, 16, 16, 32768], P(None, None, None, ('sx', 'sy'))
The draws below stay inside these ranges and needn't reach their ends.
Inputs may be any that keep to these rules, and one draw needn't show every extreme that they name: `mode_x`: the 16 entries are distinct. `mode_y`: the 16 entries are distinct. `mode_z`: the 16 entries are distinct. `mode_t`: the 8 entries are distinct.
All inputs are finite; a program needn't handle non-finite values.
Results may differ from the reference program's by a relative error of at most 0.00011.
Values sent between devices are 32-bit elements; how exact they have to be, the bound alone decides.
A program may use at most 128 MiB of HBM per device.

```python
import math
import jax
import jax.numpy as jnp
from jax import lax

B = 2
C = 16
NZ = 64
NT = 16
MX = 16
MY = 16
MZ = 16
MT = 8
NX = 128
NY = 64
NMODES = 32768
N_SX = 32
N_SY = 8


def pick_modes(key, length, amount):
    key_one, key_two = jax.random.split(key)
    middle = jax.random.permutation(key_one, length - 2)[:amount - 2] + 1
    listed = jnp.concatenate([jnp.array([0, length - 1], dtype=jnp.int32), middle.astype(jnp.int32)])
    shuffle = jax.random.permutation(key_two, amount)
    return listed[shuffle].astype(jnp.int32)


def draw_mode_x(key, part):
    key = jax.random.fold_in(key, 11)
    return pick_modes(key, NX, MX)


def draw_mode_y(key, part):
    key = jax.random.fold_in(key, 23)
    return pick_modes(key, NY, MY)


def draw_mode_z(key, part):
    key = jax.random.fold_in(key, 37)
    return pick_modes(key, NZ, MZ)


def draw_mode_t(key, part):
    key = jax.random.fold_in(key, 41)
    return pick_modes(key, NT, MT)


def block_levels(key, dims, cuts, smallest, high):
    def one(dim, blocks):
        steps = jax.random.uniform(jax.random.fold_in(jax.random.fold_in(key, 6), dim), (blocks,), jnp.float32, smallest / len(cuts), high / len(cuts))
        return jnp.repeat(jnp.exp(steps), dims[dim] // blocks).reshape((-1,) + (1,) * (len(dims) - dim - 1))

    loudness = one(*cuts[0])
    for cut in cuts[1:]:
        loudness = loudness * one(*cut)
    return loudness


def bell_draw(rng, shape, deviation, most, shards=(), held_as=jnp.bfloat16):
    drawn = jax.random.normal(rng, shape, jnp.float32) * deviation
    if len(shards) > 0:
        drawn = block_levels(rng, shape, shards, -0.22, 0.18) * drawn
    return jnp.clip(drawn, min=-most, max=most).astype(held_as)


def setup_inputs(seed: int = 0) -> dict:
    key_of = jax.random.split(jax.random.key(seed), 9)
    return {
        "field": bell_draw(key_of[0], (B, C, NX, NY, NZ * NT), 1.0, 6.0, ((2, 32), (3, 8)), jnp.float32),
        "grad_out": bell_draw(key_of[1], (B, C, NX, NY, NZ * NT), 1.0, 6.0, ((2, 32), (3, 8)), jnp.float32),
        "local_weight": bell_draw(key_of[2], (C, C), C ** -0.5, 1.5, (), jnp.float32),
        "mode_weight": bell_draw(key_of[3], (2, C, C, NMODES), (2 * C) ** -0.5, 1.0, ((3, 256),), jnp.float32),
        "mode_x": draw_mode_x(jax.random.fold_in(key_of[8], 71), 0),
        "mode_y": draw_mode_y(jax.random.fold_in(key_of[8], 71), 0),
        "mode_z": draw_mode_z(jax.random.fold_in(key_of[8], 71), 0),
        "mode_t": draw_mode_t(jax.random.fold_in(key_of[8], 71), 0),
    }


def gelu_slope(values):
    normal_cdf = 0.5 * (1.0 + jax.scipy.special.erf(values * (1.0 / math.sqrt(2.0))))
    density = jnp.exp(-0.5 * values * values) * (1.0 / math.sqrt(2.0 * math.pi))
    return normal_cdf + values * density

def pack_modes(stacked):
    zt_block = MZ * MT // N_SX
    kx_block = MX // N_SY
    shaped = stacked.reshape(2, B, C, N_SX, zt_block, N_SY, kx_block, MY)
    shaped = jnp.transpose(shaped, (0, 1, 2, 3, 5, 4, 6, 7))
    return shaped.reshape(2, B, C, MX * MY * MZ * MT)

def unpack_modes(packed):
    zt_block = MZ * MT // N_SX
    kx_block = MX // N_SY
    shaped = packed.reshape(2, B, C, N_SX, N_SY, zt_block, kx_block, MY)
    shaped = jnp.transpose(shaped, (0, 1, 2, 3, 5, 4, 6, 7))
    return shaped.reshape(2, B, C, MZ, MT, MX, MY)

def reference(field, grad_out, local_weight, mode_weight, mode_x, mode_y, mode_z, mode_t):
    total_cells = NX * NY * NZ * NT
    forward_scale = 1.0 / math.sqrt(total_cells)
    inverse_scale = 1.0 / math.sqrt(MX * MY * MZ * MT)
    highest = lax.Precision.HIGHEST

    def transform(values, factor):
        shaped = values.reshape(B, C, NX, NY, NZ, NT)

        def channel(channel_data):
            spectra = jnp.fft.fftn(channel_data, axes=(1, 2, 3, 4))
            spectra = jnp.take(spectra, mode_x, axis=1)
            spectra = jnp.take(spectra, mode_y, axis=2)
            spectra = jnp.take(spectra, mode_z, axis=3)
            spectra = jnp.take(spectra, mode_t, axis=4)
            return jnp.stack([spectra.real, spectra.imag])
        stacked = lax.map(channel, jnp.moveaxis(shaped, 1, 0))
        stacked = jnp.transpose(stacked, (1, 2, 0, 5, 6, 3, 4))
        return pack_modes(stacked) * factor

    def untransform(spectrum, factor):
        shaped = unpack_modes(spectrum)
        shaped = jnp.transpose(shaped, (2, 0, 1, 5, 6, 3, 4))
        targets = (slice(None), mode_x[:, None, None, None], mode_y[None, :, None, None], mode_z[None, None, :, None], mode_t[None, None, None, :])

        def channel(channel_data):
            blank_grid = jnp.zeros((B, NX, NY, NZ, NT), channel_data.dtype)
            real_full = blank_grid.at[targets].set(channel_data[0])
            imag_full = blank_grid.at[targets].set(channel_data[1])
            spatial = jnp.fft.ifftn(real_full + 1j * imag_full, axes=(1, 2, 3, 4))
            return spatial.real * (total_cells * factor)
        result = lax.map(channel, shaped)
        return jnp.moveaxis(result, 0, 1).reshape(B, C, NX, NY, NZ * NT)
    spectrum = transform(field, forward_scale)
    x_real, x_imag = (spectrum[0], spectrum[1])
    weight_real, weight_imag = (mode_weight[0], mode_weight[1])
    y_real = jnp.einsum('bcm,com->bom', x_real, weight_real, precision=highest) - jnp.einsum('bcm,com->bom', x_imag, weight_imag, precision=highest)
    y_imag = jnp.einsum('bcm,com->bom', x_imag, weight_real, precision=highest) + jnp.einsum('bcm,com->bom', x_real, weight_imag, precision=highest)
    spectral = untransform(jnp.stack([y_real, y_imag]), inverse_scale)
    local_term = jnp.einsum('bcxys,co->boxys', field, local_weight, precision=highest)
    hidden = spectral + local_term
    upstream = grad_out * gelu_slope(hidden)
    grad_mixed = transform(upstream, inverse_scale)
    dy_real, dy_imag = (grad_mixed[0], grad_mixed[1])
    dx_real = jnp.einsum('bom,com->bcm', dy_real, weight_real, precision=highest) + jnp.einsum('bom,com->bcm', dy_imag, weight_imag, precision=highest)
    dx_imag = jnp.einsum('bom,com->bcm', dy_imag, weight_real, precision=highest) - jnp.einsum('bom,com->bcm', dy_real, weight_imag, precision=highest)
    gw_real = jnp.einsum('bcm,bom->com', x_real, dy_real, precision=highest) + jnp.einsum('bcm,bom->com', x_imag, dy_imag, precision=highest)
    gw_imag = jnp.einsum('bcm,bom->com', x_real, dy_imag, precision=highest) - jnp.einsum('bcm,bom->com', x_imag, dy_real, precision=highest)
    grad_input = untransform(jnp.stack([dx_real, dx_imag]), forward_scale) + jnp.einsum('boxys,co->bcxys', upstream, local_weight, precision=highest)
    return (grad_input, jnp.stack([gw_real, gw_imag]))
```

```python
import functools
import math

import jax
import jax.numpy as jnp
from jax import lax
from jax.experimental import pallas as pl
from jax.experimental.pallas import tpu as pltpu
from jax.sharding import PartitionSpec as P

MESH = pl.DeviceIdType.MESH
F32 = jnp.float32
BF16 = jnp.bfloat16
NSX = 32
NSY = 8
FORWARD = 1.0 / math.sqrt(128 * 64 * 1024)
INVERSE = 1.0 / math.sqrt(32768)
ROOT_HALF = 1.0 / math.sqrt(2.0)
DENSITY = 1.0 / math.sqrt(2.0 * math.pi)


def iota(shape, dim):
    return lax.broadcasted_iota(jnp.int32, shape, dim)


def split(values):
    high = values.astype(BF16)
    return high, (values - high.astype(F32)).astype(BF16)


def dot(a, b, contract=(1, 0)):
    return lax.dot_general(
        a, b, (((contract[0],), (contract[1],)), ((), ())), preferred_element_type=F32
    )


def dot3(a_high, a_low, b_high, b_low, contract=(1, 0)):
    total = dot(a_high, b_high, contract)
    total += dot(a_high, b_low, contract)
    return total + dot(a_low, b_high, contract)


def mul3(a, b):
    return dot3(*split(a), *split(b))


def turn(phase, length):
    angle = phase.astype(F32) * (2.0 * math.pi / length)
    return jnp.cos(angle), jnp.sin(angle)


def pick(index, mode_ref, count):
    total = jnp.zeros(index.shape, jnp.int32)
    for k in range(count):
        total = jnp.where(index == k, mode_ref[k], total)
    return total


def tables_kernel(
    mx_ref, my_ref, mz_ref, mt_ref, lw_ref, th_ref, tl_ref, tx_ref, txi_ref, ty_ref, tyi_ref, kf_ref, kb_ref
):
    pair = iota((64, 128), 1)
    cz, sz = turn((iota((64, 128), 0) * pick(pair // 8, mz_ref, 16)) & 63, 64)
    pair = iota((16, 128), 1)
    ct, st = turn((iota((16, 128), 0) * pick(pair % 8, mt_ref, 8)) & 15, 16)
    cz, sz = cz[:, None, :], sz[:, None, :]
    real = (cz * ct - sz * st).reshape(1024, 128)
    imag = (-(sz * ct) - cz * st).reshape(1024, 128)
    high, low = split(real)
    th_ref[:, :128] = high
    tl_ref[:, :128] = low
    high, low = split(imag)
    th_ref[:, 128:] = high
    tl_ref[:, 128:] = low
    row, col = iota((64, 256), 0), iota((64, 256), 1)
    c, s = turn(((col // 2) * pick((row // 8) * 2 + (row // 2) % 2, mx_ref, 16)) & 127, 128)
    ro, ri = row % 2, col % 2
    value = jnp.where(ro == ri, c, jnp.where(ro == 0, s, -s))
    tx_ref[...] = jnp.where(row % 8 < 4, value, 0.0)
    row, col = iota((256, 64), 0), iota((256, 64), 1)
    c, s = turn(((row // 2) * pick((col // 8) * 2 + (col // 2) % 2, mx_ref, 16)) & 127, 128)
    ro, ri = row % 2, col % 2
    value = jnp.where(ro == ri, c, jnp.where(ro == 0, -s, s))
    txi_ref[...] = jnp.where(col % 8 < 4, value, 0.0)
    row, col = iota((128, 256), 0), iota((128, 256), 1)
    c, s = turn(((col % 64) * pick(row % 16, my_ref, 16)) & 63, 64)
    same = (row // 64 == col // 128) & ((row // 16) % 2 == (col // 64) % 2)
    ty_ref[...] = jnp.where(same, jnp.where((row // 32) % 2 == 0, c, s), 0.0)
    row, col = iota((512, 128), 0), iota((512, 128), 1)
    y = ((row // 32) % 8) * 8 + row % 8
    c, s = turn((y * pick(col % 16, my_ref, 16)) & 63, 64)
    ro, ri = row // 256, (col // 32) % 2
    same = ((row // 8) % 2 == col // 64) & ((row // 16) % 2 == (col // 16) % 2)
    value = jnp.where(ro == ri, c, jnp.where(ro == 0, -s, s))
    tyi_ref[...] = jnp.where(same, value, 0.0)
    row, col = iota((256, 16), 0), iota((256, 16), 1)
    spread = jnp.where(row // 16 == col, 1.0, 0.0)
    weight = lw_ref[...]
    wide = lax.dot_general(
        spread, weight, (((1,), (0,)), ((), ())), precision=lax.Precision.HIGHEST, preferred_element_type=F32
    )
    wide = lax.dot_general(
        wide, spread, (((1,), (1,)), ((), ())), precision=lax.Precision.HIGHEST, preferred_element_type=F32
    )
    row, col = iota((256, 256), 0), iota((256, 256), 1)
    wide = jnp.where(row % 16 == col % 16, wide, 0.0)
    kb_ref[...] = wide
    kf_ref[...] = wide.T


def make_tables(mode_x, mode_y, mode_z, mode_t, local_weight):
    shape = jax.ShapeDtypeStruct
    smem = pl.BlockSpec(memory_space=pltpu.SMEM)
    vmem = pl.BlockSpec(memory_space=pltpu.VMEM)
    return pl.pallas_call(
        tables_kernel,
        out_shape=(
            shape((1024, 256), BF16),
            shape((1024, 256), BF16),
            shape((64, 256), F32),
            shape((256, 64), F32),
            shape((128, 256), F32),
            shape((512, 128), F32),
            shape((256, 256), F32),
            shape((256, 256), F32),
        ),
        in_specs=[smem, smem, smem, smem, vmem],
        out_specs=[vmem] * 8,
        compiler_params=pltpu.CompilerParams(vmem_limit_bytes=24 << 20),
        name="tables",
    )(mode_x, mode_y, mode_z, mode_t, local_weight)


def swap_lanes(first, second, width):
    low = (iota(first.shape, 1) // width) % 2 == 0
    return (
        jnp.where(low, first, pltpu.roll(second, width, 1)),
        jnp.where(low, pltpu.roll(first, 128 - width, 1), second),
    )


def swap_four(parts):
    a, b, c, d = parts
    a, c = swap_lanes(a, c, 64)
    b, d = swap_lanes(b, d, 64)
    a, b = swap_lanes(a, b, 32)
    c, d = swap_lanes(c, d, 32)
    return a, b, c, d


def gelu_slope(values):
    normal_cdf = 0.5 * (1.0 + lax.erf(values * ROOT_HALF))
    return normal_cdf + values * (jnp.exp(-0.5 * values * values) * DENSITY)


def chain_kernel(
    field_ref, gout_ref, w_ref, th_ref, tl_ref, tx_ref, txi_ref, ty_ref, tyi_ref, kf_ref,
    uh_out, ul_out, last_out, gm_ref,
    field, gout, fh, fl, uh, ul, sa, ra, sb, rb, sc, rc, turned, spectra, slopes, mixed,
    load_sem, store_sem, sa_send, sa_recv, sa_own, sb_send, sb_recv, sb_own, sc_send, sc_recv, sc_own,
):
    sx, sy = lax.axis_index("sx"), lax.axis_index("sy")

    def load(b, which):
        source, target = ((field_ref, field), (gout_ref, gout))[which]
        return pltpu.make_async_copy(source.at[b], target.at[b], load_sem.at[which, b])

    for which in range(2):
        for b in range(2):
            load(b, which).start()

    barrier = pltpu.get_barrier_semaphore()

    def greet(axis, me, n):
        def one(d, carry):
            pl.semaphore_signal(
                barrier, inc=1, device_id={axis: lax.rem(me + d, n)}, device_id_type=MESH
            )
            return carry

        lax.fori_loop(1, n, one, 0)

    greet("sy", sy, NSY)
    greet("sx", sx, NSX)

    def exchange(axis, me, n, source, target, send, recv, own):
        def one(d, carry):
            to = lax.rem(me + d, n)
            pltpu.make_async_remote_copy(
                src_ref=source(to),
                dst_ref=target(me),
                send_sem=send,
                recv_sem=recv,
                device_id={axis: to},
                device_id_type=MESH,
            ).start()
            return carry

        lax.fori_loop(1, n, one, 0)
        pltpu.make_async_copy(source(me), target(me), own).start()

    def drain(whole, one, sem, own=None):
        pltpu.make_async_copy(whole, whole, sem).wait()
        if own is not None:
            pltpu.make_async_copy(one, one, own).wait()

    def start_a(k, b):
        target = (lambda d: ra.at[k, b, d]) if k < 3 else (lambda d: last_out.at[b, d])
        exchange(
            "sy", sy, NSY, lambda d: sa.at[k, b, d], target, sa_send.at[k, b], sa_recv.at[k, b], sa_own.at[k, b]
        )

    def wait_a(k, b):
        whole = ra.at[k, b] if k < 3 else last_out.at[b]
        drain(whole.at[pl.ds(0, NSY - 1)], whole.at[0], sa_recv.at[k, b], sa_own.at[k, b])

    def start_b(k, b):
        rows = lambda d: pl.ds(pl.multiple_of(d * 8, 8), 8)
        exchange(
            "sx", sx, NSX, lambda d: sb.at[k, b, rows(d)], lambda d: rb.at[k, b, rows(d)],
            sb_send.at[k, b], sb_recv.at[k, b], sb_own.at[k, b],
        )

    def wait_b(k, b):
        whole = rb.at[k, b]
        drain(whole.at[pl.ds(0, (NSX - 1) * 8)], whole.at[pl.ds(0, 8)], sb_recv.at[k, b], sb_own.at[k, b])

    def start_c(k, b):
        rows = lambda d: pl.ds(pl.multiple_of(d * 8, 8), 8)
        exchange(
            "sy", sy, NSY, lambda d: sc.at[k, b, rows(d)], lambda d: rc.at[k, b, rows(d)],
            sc_send.at[k, b], sc_recv.at[k, b], sc_own.at[k, b],
        )

    def wait_c(k, b):
        whole = rc.at[k, b]
        drain(whole.at[pl.ds(0, (NSY - 1) * 8)], whole.at[pl.ds(0, 8)], sc_recv.at[k, b], sc_own.at[k, b])

    def zt_forward(k, b, high_ref, low_ref, source=None):
        def block(m, carry):
            rows = pl.ds(m * 8, 8)
            if source is None:
                high = high_ref[b, rows].reshape(256, 1024)
                low = low_ref[b, rows].reshape(256, 1024)
            else:
                high, low = split(source[b, rows].reshape(256, 1024))
                high_ref[b, rows] = high.reshape(8, 32, 1024)
                low_ref[b, rows] = low.reshape(8, 32, 1024)
            out = dot3(high, low, th_ref[...], tl_ref[...])
            sa[k, b, pl.ds(m * 4, 4)] = out.reshape(4, 64, 256)
            return carry

        lax.fori_loop(0, 2, block, 0)

    def y_forward(ka, kb, b):
        for i in range(2):
            parts = [
                ra[ka, b, :, c * 32 + (i * 2 + x) * 8 : c * 32 + (i * 2 + x) * 8 + 8, :].reshape(64, 256)
                for x in range(2)
                for c in range(2)
            ]
            out = mul3(ty_ref[...], jnp.concatenate(parts, axis=0))
            rows = []
            for x in range(2):
                cos, sin = out[x * 64 : x * 64 + 32], out[x * 64 + 32 : x * 64 + 64]
                rows.append(cos[:, :128] + sin[:, 128:])
                rows.append(cos[:, 128:] - sin[:, :128])
            turned[i] = jnp.concatenate(rows, axis=0).T
            parts = swap_four([turned[i, pl.ds(z, 32, stride=4), :] for z in range(4)])
            for q in range(4):
                sb[kb, b, pl.ds(i * 4 + q, 32, stride=8), :] = parts[q]

    def y_backward(kb, ka, b):
        halves = []
        for i in range(2):
            parts = swap_four([rb[kb, b, pl.ds(i * 4 + q, 32, stride=8), :] for q in range(4)])
            for z in range(4):
                turned[i, pl.ds(z, 32, stride=4), :] = parts[z]
            halves.append(turned[i].T)
        out = mul3(tyi_ref[...], jnp.concatenate(halves, axis=1))
        for part in range(2):
            for i in range(2):
                block = out[part * 256 : part * 256 + 256, i * 128 : i * 128 + 128].reshape(8, 2, 16, 128)
                for o in range(2):
                    sa[ka, b, :, o * 32 + i * 16 : o * 32 + i * 16 + 16, part * 128 : part * 128 + 128] = block[:, o]

    def x_forward(kb, kc, b):
        sc[kc, b] = mul3(tx_ref[...], rb[kb, b])

    def x_backward(kc, kb, b):
        sb[kb, b] = mul3(txi_ref[...], rc[kc, b])

    def gather_modes(kc, b, keep, factor):
        for part in range(2):
            pair = swap_lanes(
                rc[kc, b, pl.ds(part, 8, stride=8), :], rc[kc, b, pl.ds(2 + part, 8, stride=8), :], 16
            )
            for low in range(2):
                keep[b, part, pl.ds(low, 8, stride=2), :] = pair[low] * factor

    def spread_modes(kc, b):
        for part in range(2):
            pair = swap_lanes(
                mixed[part, pl.ds(0, 8, stride=2), :], mixed[part, pl.ds(1, 8, stride=2), :], 16
            )
            for kx in range(2):
                sc[kc, b, pl.ds(kx * 2 + part, 8, stride=8), :] = pair[kx]
        for idle in range(4, 8):
            sc[kc, b, pl.ds(idle, 8, stride=8), :] = jnp.zeros((8, 128), F32)

    def mix(kin, kout, b):
        gather_modes(kin, b, spectra, FORWARD)

        def channel(c, carry):
            real, imag = carry
            wr, wi = w_ref[0, c], w_ref[1, c]
            xr, xi = spectra[b, 0, pl.ds(c, 1), :], spectra[b, 1, pl.ds(c, 1), :]
            return real + (wr * xr - wi * xi), imag + (wr * xi + wi * xr)

        zero = jnp.zeros((16, 128), F32)
        real, imag = lax.fori_loop(0, 16, channel, (zero, zero), unroll=4)
        mixed[0] = real * INVERSE
        mixed[1] = imag * INVERSE
        spread_modes(kout, b)

    def mix_back(kin, kout, b):
        gather_modes(kin, b, slopes, INVERSE)
        dr, di = slopes[b, 0], slopes[b, 1]

        def channel(c, carry):
            wr, wi = w_ref[0, c], w_ref[1, c]
            mixed[0, pl.ds(c, 1), :] = jnp.sum(wr * dr + wi * di, axis=0, keepdims=True) * FORWARD
            mixed[1, pl.ds(c, 1), :] = jnp.sum(wr * di - wi * dr, axis=0, keepdims=True) * FORWARD
            return carry

        lax.fori_loop(0, 16, channel, 0, unroll=4)
        spread_modes(kout, b)

    def weight_grad():
        def channel(c, carry):
            real = imag = jnp.zeros((16, 128), F32)
            for b in range(2):
                xr, xi = spectra[b, 0, pl.ds(c, 1), :], spectra[b, 1, pl.ds(c, 1), :]
                dr, di = slopes[b, 0], slopes[b, 1]
                real = real + (xr * dr + xi * di)
                imag = imag + (xr * di - xi * dr)
            gm_ref[0, c] = real
            gm_ref[1, c] = imag
            return carry

        lax.fori_loop(0, 16, channel, 0)

    def slope_stage(ka, b):
        for g in range(2):
            cells = slice(g * 16, g * 16 + 16)
            parts = [ra[ka, b, :, o * 32 + g * 16 : o * 32 + g * 16 + 16, :] for o in range(2)]
            lh, ll = split(jnp.concatenate(parts, axis=1).reshape(256, 256))
            kh, kl = split(kf_ref[...])

            def columns(n, carry):
                cols = pl.ds(pl.multiple_of(n * 256, 256), 256)
                hidden = dot3(lh, ll, th_ref[cols, :], tl_ref[cols, :], (1, 1))
                hidden += dot3(
                    kh, kl, fh[b, :, cells, cols].reshape(256, 256), fl[b, :, cells, cols].reshape(256, 256)
                )
                upstream = gout[b, :, cells, cols].reshape(256, 256) * gelu_slope(hidden)
                high, low = split(upstream)
                uh[b, :, cells, cols] = high.reshape(16, 16, 256)
                ul[b, :, cells, cols] = low.reshape(16, 16, 256)
                return carry

            lax.fori_loop(0, 4, columns, 0)

    def store(b):
        return (
            pltpu.make_async_copy(uh.at[b], uh_out.at[b], store_sem.at[0, b]),
            pltpu.make_async_copy(ul.at[b], ul_out.at[b], store_sem.at[1, b]),
        )

    for b in range(2):
        load(b, 0).wait()
        zt_forward(0, b, fh, fl, field)
        if b == 0:
            pl.semaphore_wait(barrier, NSX + NSY - 2)
        start_a(0, b)
    for b in range(2):
        wait_a(0, b)
        y_forward(0, 0, b)
        start_b(0, b)
    for b in range(2):
        wait_b(0, b)
        x_forward(0, 0, b)
        start_c(0, b)
    for b in range(2):
        wait_c(0, b)
        mix(0, 1, b)
        start_c(1, b)
    for b in range(2):
        wait_c(1, b)
        x_backward(1, 1, b)
        start_b(1, b)
    for b in range(2):
        wait_b(1, b)
        y_backward(1, 1, b)
        start_a(1, b)
    for b in range(2):
        wait_a(1, b)
        load(b, 1).wait()
        slope_stage(1, b)
        zt_forward(2, b, uh, ul)
        start_a(2, b)
        for copy in store(b):
            copy.start()
    for b in range(2):
        wait_a(2, b)
        y_forward(2, 2, b)
        start_b(2, b)
    for b in range(2):
        wait_b(2, b)
        x_forward(2, 2, b)
        start_c(2, b)
    for b in range(2):
        wait_c(2, b)
        mix_back(2, 3, b)
        start_c(3, b)
    for b in range(2):
        wait_c(3, b)
        x_backward(3, 3, b)
        start_b(3, b)
    weight_grad()
    for b in range(2):
        wait_b(3, b)
        y_backward(3, 3, b)
        start_a(3, b)
    for b in range(2):
        wait_a(3, b)
    for b in range(2):
        for k in range(4):
            drain(sa.at[k, b, pl.ds(0, NSY - 1)], None, sa_send.at[k, b])
            drain(sb.at[k, b, pl.ds(0, (NSX - 1) * 8)], None, sb_send.at[k, b])
            drain(sc.at[k, b, pl.ds(0, (NSY - 1) * 8)], None, sc_send.at[k, b])
        for copy in store(b):
            copy.wait()


def chain(field, gout, weight, th, tl, tx, txi, ty, tyi, kf):
    shape = jax.ShapeDtypeStruct
    any_space = pl.BlockSpec(memory_space=pl.ANY)
    vmem = pl.BlockSpec(memory_space=pltpu.VMEM)
    sems = pltpu.SemaphoreType.DMA
    return pl.pallas_call(
        chain_kernel,
        out_shape=(
            shape((2, 16, 32, 1024), BF16),
            shape((2, 16, 32, 1024), BF16),
            shape((2, 8, 64, 256), F32),
            shape((2, 16, 16, 128), F32),
        ),
        in_specs=[any_space] * 2 + [vmem] * 8,
        out_specs=[any_space, any_space, any_space, vmem],
        scratch_shapes=[
            pltpu.VMEM((2, 16, 32, 1024), F32),
            pltpu.VMEM((2, 16, 32, 1024), F32),
            pltpu.VMEM((2, 16, 32, 1024), BF16),
            pltpu.VMEM((2, 16, 32, 1024), BF16),
            pltpu.VMEM((2, 16, 32, 1024), BF16),
            pltpu.VMEM((2, 16, 32, 1024), BF16),
            pltpu.VMEM((4, 2, 8, 64, 256), F32),
            pltpu.VMEM((3, 2, 8, 64, 256), F32),
            pltpu.VMEM((4, 2, 256, 128), F32),
            pltpu.VMEM((4, 2, 256, 128), F32),
            pltpu.VMEM((4, 2, 64, 128), F32),
            pltpu.VMEM((4, 2, 64, 128), F32),
            pltpu.VMEM((2, 128, 128), F32),
            pltpu.VMEM((2, 2, 16, 128), F32),
            pltpu.VMEM((2, 2, 16, 128), F32),
            pltpu.VMEM((2, 16, 128), F32),
            sems((2, 2)),
            sems((2, 2)),
        ]
        + [sems((4, 2))] * 9,
        compiler_params=pltpu.CompilerParams(
            collective_id=1, has_side_effects=True, vmem_limit_bytes=56 << 20
        ),
        name="chain",
    )(field, gout, weight, th, tl, tx, txi, ty, tyi, kf)


def finish_kernel(spectra_ref, uh_ref, ul_ref, th_ref, tl_ref, kb_ref, out_ref):
    parts = [spectra_ref[0, :, o, :, :] for o in range(2)]
    lh, ll = split(jnp.concatenate(parts, axis=1).reshape(256, 256))
    kh, kl = split(kb_ref[...])

    def columns(n, carry):
        cols = pl.ds(pl.multiple_of(n * 256, 256), 256)
        total = dot3(lh, ll, th_ref[cols, :], tl_ref[cols, :], (1, 1))
        total += dot3(
            kh, kl, uh_ref[0, :, :, cols].reshape(256, 256), ul_ref[0, :, :, cols].reshape(256, 256)
        )
        out_ref[0, :, :, cols] = total.reshape(16, 16, 256)
        return carry

    lax.fori_loop(0, 4, columns, 0)


def finish(spectra, uh, ul, th, tl, kb):
    cells = pl.BlockSpec((1, 16, 16, 1024), lambda b, g: (b, 0, g, 0))
    fixed = lambda *shape: pl.BlockSpec(shape, lambda b, g: (0,) * len(shape))
    return pl.pallas_call(
        finish_kernel,
        grid=(2, 2),
        out_shape=jax.ShapeDtypeStruct((2, 16, 32, 1024), F32),
        in_specs=[
            pl.BlockSpec((1, 8, 2, 16, 256), lambda b, g: (b, 0, 0, g, 0)),
            cells,
            cells,
            fixed(1024, 256),
            fixed(1024, 256),
            fixed(256, 256),
        ],
        out_specs=cells,
        compiler_params=pltpu.CompilerParams(vmem_limit_bytes=32 << 20),
        name="finish",
    )(spectra.reshape(2, 8, 2, 32, 256), uh, ul, th, tl, kb)


def body(field, grad_out, local_weight, mode_weight, mode_x, mode_y, mode_z, mode_t):
    th, tl, tx, txi, ty, tyi, kf, kb = make_tables(mode_x, mode_y, mode_z, mode_t, local_weight)
    uh, ul, spectra, grad_modes = chain(
        field.reshape(2, 16, 32, 1024),
        grad_out.reshape(2, 16, 32, 1024),
        mode_weight,
        th, tl, tx, txi, ty, tyi, kf,
    )
    grad_input = finish(spectra, uh, ul, th, tl, kb)
    return grad_input.reshape(field.shape), grad_modes


def solution(mesh):
    grid = P(None, None, "sx", "sy", None)
    modes = P(None, None, None, ("sx", "sy"))
    return jax.shard_map(
        body,
        mesh=mesh,
        in_specs=(grid, grid, P(), modes, P(), P(), P(), P()),
        out_specs=(grid, modes),
        check_vma=False,
    )
```

```python
import functools
import math

import jax
import jax.numpy as jnp
from jax import lax
from jax.experimental import pallas as pl
from jax.experimental.pallas import tpu as pltpu
from jax.sharding import PartitionSpec as P

MESH = pl.DeviceIdType.MESH
F32 = jnp.float32
BF16 = jnp.bfloat16
NSX = 32
NSY = 8
FORWARD = 1.0 / math.sqrt(128 * 64 * 1024)
INVERSE = 1.0 / math.sqrt(32768)
ROOT_HALF = 1.0 / math.sqrt(2.0)
DENSITY = 1.0 / math.sqrt(2.0 * math.pi)


def iota(shape, dim):
    return lax.broadcasted_iota(jnp.int32, shape, dim)


def split(values):
    high = values.astype(BF16)
    return high, (values - high.astype(F32)).astype(BF16)


def dot(a, b, contract=(1, 0)):
    return lax.dot_general(
        a, b, (((contract[0],), (contract[1],)), ((), ())), preferred_element_type=F32
    )


def dot3(a_high, a_low, b_high, b_low, contract=(1, 0)):
    total = dot(a_high, b_high, contract)
    total += dot(a_high, b_low, contract)
    return total + dot(a_low, b_high, contract)


def mul3(a, b):
    return dot3(*split(a), *split(b))


def turn(phase, length):
    angle = phase.astype(F32) * (2.0 * math.pi / length)
    return jnp.cos(angle), jnp.sin(angle)


def pick(index, mode_ref, count):
    total = jnp.zeros(index.shape, jnp.int32)
    for k in range(count):
        total = jnp.where(index == k, mode_ref[k], total)
    return total


def build_zt(mz_ref, mt_ref, th_ref, tl_ref):
    pair = iota((64, 128), 1)
    cz, sz = turn((iota((64, 128), 0) * pick(pair // 8, mz_ref, 16)) & 63, 64)
    pair = iota((16, 128), 1)
    ct, st = turn((iota((16, 128), 0) * pick(pair % 8, mt_ref, 8)) & 15, 16)
    cz, sz = cz[:, None, :], sz[:, None, :]
    real = (cz * ct - sz * st).reshape(1024, 128)
    imag = (-(sz * ct) - cz * st).reshape(1024, 128)
    th_ref[:, :128], tl_ref[:, :128] = split(real)
    th_ref[:, 128:], tl_ref[:, 128:] = split(imag)


def build_y(my_ref, ty_ref):
    row, col = iota((128, 256), 0), iota((128, 256), 1)
    c, s = turn(((col % 64) * pick(row % 16, my_ref, 16)) & 63, 64)
    same = (row // 64 == col // 128) & ((row // 16) % 2 == (col // 64) % 2)
    ty_ref[...] = jnp.where(same, jnp.where((row // 32) % 2 == 0, c, s), 0.0)


def build_y_back(my_ref, tyi_ref):
    row, col = iota((512, 128), 0), iota((512, 128), 1)
    y = ((row // 32) % 8) * 8 + row % 8
    c, s = turn((y * pick(col % 16, my_ref, 16)) & 63, 64)
    ro, ri = row // 256, (col // 32) % 2
    same = ((row // 8) % 2 == col // 64) & ((row // 16) % 2 == (col // 16) % 2)
    value = jnp.where(ro == ri, c, jnp.where(ro == 0, -s, s))
    tyi_ref[...] = jnp.where(same, value, 0.0)


def build_x(mx_ref, tx_ref):
    row, col = iota((64, 256), 0), iota((64, 256), 1)
    c, s = turn(((col // 2) * pick((row // 8) * 2 + (row // 2) % 2, mx_ref, 16)) & 127, 128)
    ro, ri = row % 2, col % 2
    value = jnp.where(ro == ri, c, jnp.where(ro == 0, s, -s))
    tx_ref[...] = jnp.where(row % 8 < 4, value, 0.0)


def build_x_back(mx_ref, txi_ref):
    row, col = iota((256, 32), 0), iota((256, 32), 1)
    c, s = turn(((row // 2) * pick(col // 2, mx_ref, 16)) & 127, 128)
    ro, ri = row % 2, col % 2
    txi_ref[...] = jnp.where(ro == ri, c, jnp.where(ro == 0, -s, s))


def build_maps(lw_ref, kf_ref, kb_ref):
    row, col = iota((256, 16), 0), iota((256, 16), 1)
    spread = jnp.where(row // 16 == col, 1.0, 0.0)
    high = lax.Precision.HIGHEST
    wide = lax.dot_general(
        spread, lw_ref[...], (((1,), (0,)), ((), ())), precision=high, preferred_element_type=F32
    )
    wide = lax.dot_general(
        wide, spread, (((1,), (1,)), ((), ())), precision=high, preferred_element_type=F32
    )
    row, col = iota((256, 256), 0), iota((256, 256), 1)
    wide = jnp.where(row % 16 == col % 16, wide, 0.0)
    kb_ref[...] = wide
    kf_ref[...] = wide.T


SY_PEERS = ((2, 1), (1, 1), (3, 1), (2, 0), (0, 1), (1, 0), (3, 0))


def swap_lanes(first, second, width):
    low = (iota(first.shape, 1) // width) % 2 == 0
    return (
        jnp.where(low, first, pltpu.roll(second, width, 1)),
        jnp.where(low, pltpu.roll(first, 128 - width, 1), second),
    )


def swap_four(parts):
    a, b, c, d = parts
    a, c = swap_lanes(a, c, 64)
    b, d = swap_lanes(b, d, 64)
    a, b = swap_lanes(a, b, 32)
    c, d = swap_lanes(c, d, 32)
    return a, b, c, d


def gelu_slope(values):
    normal_cdf = 0.5 * (1.0 + lax.erf(values * ROOT_HALF))
    return normal_cdf + values * (jnp.exp(-0.5 * values * values) * DENSITY)


def chain_kernel(
    field_ref, gout_ref, w_hbm, lw_hbm, mx_hbm, my_hbm, mz_hbm, mt_hbm,
    local_out, last_out, th_out, tl_out, gm_out,
    field, gout, fh, fl, sa, ra, sb, rb, sc, rc, sd, rd, ws, wr, turned, spectra, slopes,
    w_ref, lw_ref, th_ref, tl_ref, tx_ref, txi_ref, ty_ref, tyi_ref, kf_ref, kb_ref, gm_ref,
    mx_ref, my_ref, mz_ref, mt_ref,
    load_sem, small_sem, store_sem, sa_send, sa_recv, sa_own, sb_send, sb_recv, sb_own,
    sc_send, sc_recv, sc_own, sd_send, sd_recv, sd_own, w_send, w_recv, w_own,
):
    sx, sy = lax.axis_index("sx"), lax.axis_index("sy")

    def load(b, which):
        source, target = ((field_ref, field), (gout_ref, gout))[which]
        return pltpu.make_async_copy(source.at[b], target.at[b], load_sem.at[which, b])

    def small(i):
        source = (mz_hbm, mt_hbm, mx_hbm, my_hbm, lw_hbm, w_hbm)[i]
        target = (mz_ref, mt_ref, mx_ref, my_ref, lw_ref, w_ref)[i]
        return pltpu.make_async_copy(source, target, small_sem.at[i])

    def store(i):
        source = (gout.at[0], gout.at[1], th_ref, tl_ref, gm_ref)[i]
        target = (local_out.at[0], local_out.at[1], th_out, tl_out, gm_out)[i]
        return pltpu.make_async_copy(source, target, store_sem.at[i])

    small(0).start()
    small(1).start()
    load(0, 0).start()
    barrier = pltpu.get_barrier_semaphore()

    def greet(axis, me, n):
        def one(d, carry):
            pl.semaphore_signal(
                barrier, inc=1, device_id={axis: lax.rem(me + d, n)}, device_id_type=MESH
            )
            return carry

        lax.fori_loop(1, n, one, 0)

    greet("sy", sy, NSY)
    greet("sx", sx, NSX)
    for i in range(2, 6):
        small(i).start()
    load(1, 0).start()
    load(0, 1).start()
    load(1, 1).start()

    def send(axis, to, source, target, sems):
        pltpu.make_async_remote_copy(
            src_ref=source,
            dst_ref=target,
            send_sem=sems[0],
            recv_sem=sems[1],
            device_id={axis: to},
            device_id_type=MESH,
        ).start()

    def over_sy(source, target, sems):
        for dy, dx in SY_PEERS:
            to = lax.rem(sy // 2 + dy, 4) * 2 + lax.rem(sy + dx, 2)
            send("sy", to, source(to), target(sy), sems)
        pltpu.make_async_copy(source(sy), target(sy), sems[2]).start()

    def over_sx(source, target, sems):
        def at(dx, dz, dc):
            to = lax.rem(sx // 16 + dx, 2) * 16 + lax.rem(sx // 2 + dz, 8) * 2 + lax.rem(sx + dc, 2)
            send("sx", to, source(to), target(sx), sems)

        def ring(j, carry):
            dz = 12 + ((j + 1) // 2) * (2 * lax.rem(j, 2) - 1)
            for dx, dc in ((1, 1), (1, 0), (0, 1), (0, 0)):
                at(dx, dz, dc)
            return carry

        lax.fori_loop(0, 7, ring, 0)
        for dx, dc in ((1, 1), (1, 0), (0, 1)):
            at(dx, 0, dc)
        pltpu.make_async_copy(source(sx), target(sx), sems[2]).start()

    def drain(whole, one, sem, own=None):
        pltpu.make_async_copy(whole, whole, sem).wait()
        if own is not None:
            pltpu.make_async_copy(one, one, own).wait()

    def eight(d):
        return pl.ds(pl.multiple_of(d * 8, 8), 8)

    def start_a(k, b):
        target = (lambda d: ra.at[k, b, d]) if k < 3 else (lambda d: last_out.at[b, d])
        over_sy(lambda d: sa.at[k, b, d], target, (sa_send.at[k, b], sa_recv.at[k, b], sa_own.at[k, b]))

    def wait_a(k, b):
        whole = ra.at[k, b] if k < 3 else last_out.at[b]
        drain(whole.at[pl.ds(0, NSY - 1)], whole.at[0], sa_recv.at[k, b], sa_own.at[k, b])

    def start_b(k, b):
        over_sx(
            lambda d: sb.at[k, b, eight(d)],
            lambda d: rb.at[k, b, eight(d)],
            (sb_send.at[k, b], sb_recv.at[k, b], sb_own.at[k, b]),
        )

    def wait_b(k, b):
        whole = rb.at[k, b]
        drain(whole.at[pl.ds(0, (NSX - 1) * 8)], whole.at[pl.ds(0, 8)], sb_recv.at[k, b], sb_own.at[k, b])

    def start_c(k, b):
        over_sy(
            lambda d: sc.at[k, b, eight(d)],
            lambda d: rc.at[k, b, eight(d)],
            (sc_send.at[k, b], sc_recv.at[k, b], sc_own.at[k, b]),
        )

    def wait_c(k, b):
        whole = rc.at[k, b]
        drain(whole.at[pl.ds(0, (NSY - 1) * 8)], whole.at[pl.ds(0, 8)], sc_recv.at[k, b], sc_own.at[k, b])

    def start_d(k, b):
        over_sy(
            lambda d: sd.at[k, b, pl.ds(pl.multiple_of(d * 32, 32), 32)],
            lambda d: rd.at[k, b, d],
            (sd_send.at[k, b], sd_recv.at[k, b], sd_own.at[k, b]),
        )

    def wait_d(k, b):
        whole = rd.at[k, b]
        drain(whole.at[pl.ds(0, NSY - 1)], whole.at[0], sd_recv.at[k, b], sd_own.at[k, b])

    def start_w(k):
        over_sy(lambda d: ws.at[k, d], lambda d: wr.at[k, d], (w_send.at[k], w_recv.at[k], w_own.at[k]))

    def wait_w(k):
        whole = wr.at[k]
        drain(whole.at[pl.ds(0, NSY - 1)], whole.at[0], w_recv.at[k], w_own.at[k])

    def zt_forward(k, b, high_ref, low_ref, source=None):
        def block(m, carry):
            rows = pl.ds(m * 8, 8)
            if source is None:
                high = high_ref[b, rows].reshape(256, 1024)
                low = low_ref[b, rows].reshape(256, 1024)
            else:
                high, low = split(source[b, rows].reshape(256, 1024))
                high_ref[b, rows] = high.reshape(8, 32, 1024)
                low_ref[b, rows] = low.reshape(8, 32, 1024)
            out = dot3(high, low, th_ref[...], tl_ref[...])
            sa[k, b, pl.ds(m * 4, 4)] = out.reshape(4, 64, 256)
            return carry

        lax.fori_loop(0, 2, block, 0)

    def y_forward(ka, kb, b):
        for i in range(2):
            parts = [
                ra[ka, b, :, c * 32 + (i * 2 + x) * 8 : c * 32 + (i * 2 + x) * 8 + 8, :].reshape(64, 256)
                for x in range(2)
                for c in range(2)
            ]
            out = mul3(ty_ref[...], jnp.concatenate(parts, axis=0))
            rows = []
            for x in range(2):
                cos, sin = out[x * 64 : x * 64 + 32], out[x * 64 + 32 : x * 64 + 64]
                rows.append(cos[:, :128] + sin[:, 128:])
                rows.append(cos[:, 128:] - sin[:, :128])
            turned[i] = jnp.concatenate(rows, axis=0).T
            parts = swap_four([turned[i, pl.ds(z, 32, stride=4), :] for z in range(4)])
            for q in range(4):
                sb[kb, b, pl.ds(i * 4 + q, 32, stride=8), :] = parts[q]

    def y_backward(kb, ka, b):
        halves = []
        for i in range(2):
            parts = swap_four([rb[kb, b, pl.ds(i * 4 + q, 32, stride=8), :] for q in range(4)])
            for z in range(4):
                turned[i, pl.ds(z, 32, stride=4), :] = parts[z]
            halves.append(turned[i].T)
        out = mul3(tyi_ref[...], jnp.concatenate(halves, axis=1))
        for part in range(2):
            for i in range(2):
                block = out[part * 256 : part * 256 + 256, i * 128 : i * 128 + 128].reshape(8, 2, 16, 128)
                for o in range(2):
                    sa[ka, b, :, o * 32 + i * 16 : o * 32 + i * 16 + 16, part * 128 : part * 128 + 128] = block[:, o]

    def x_forward(kb, kc, b):
        sc[kc, b] = mul3(tx_ref[...], rb[kb, b])

    def x_backward(kd, kb, b):
        total = rd[kd, b, 0]
        for d in range(1, NSY):
            total += rd[kd, b, d]
        sb[kb, b] = mul3(txi_ref[...], total * (FORWARD * INVERSE))

    def gather_modes(kc, b, keep, factor):
        for part in range(2):
            pair = swap_lanes(
                rc[kc, b, pl.ds(part, 8, stride=8), :], rc[kc, b, pl.ds(2 + part, 8, stride=8), :], 16
            )
            for low in range(2):
                keep[b, part, pl.ds(low, 8, stride=2), :] = pair[low] * factor

    def spread_weights(k):
        inner, outer = (1, 16) if k == 0 else (16, 1)
        for part in range(2):
            for slab in range(NSY):
                for low in range(2):
                    pair = [
                        w_ref[part, pl.ds((slab * 2 + own) * outer + low * inner, 8, stride=2 * inner), :]
                        for own in range(2)
                    ]
                    pair = swap_lanes(pair[0], pair[1], 16)
                    for kx in range(2):
                        ws[k, slab, part, kx, low * 8 : low * 8 + 8, :] = pair[kx]

    def mix(kc, kd, b):
        sign = 1.0 if kd == 0 else -1.0
        low = (iota((8, 128), 1) // 16) % 2 == 0

        def fold(values):
            even, odd = values[:8], values[8:]
            return jnp.where(low, even + pltpu.roll(even, 112, 1), odd + pltpu.roll(odd, 16, 1))

        def line(i, carry):
            for kx in range(2):
                real = sc[kc, b, pl.ds(i * 8 + kx * 2, 1), :]
                imag = sc[kc, b, pl.ds(i * 8 + kx * 2 + 1, 1), :]
                w_real, w_imag = wr[kd, i, 0, kx], wr[kd, i, 1, kx]
                out_real = w_real * real - sign * (w_imag * imag)
                out_imag = w_real * imag + sign * (w_imag * real)
                sd[kd, b, pl.ds(i * 4 + kx * 2, 8, stride=32), :] = fold(out_real)
                sd[kd, b, pl.ds(i * 4 + kx * 2 + 1, 8, stride=32), :] = fold(out_imag)
            return carry

        lax.fori_loop(0, NSY, line, 0, unroll=True)

    def weight_grad():
        for b in range(2):
            wait_c(0, b)
            gather_modes(0, b, spectra, FORWARD)
            wait_c(1, b)
            gather_modes(1, b, slopes, INVERSE)

        def channel(c, carry):
            real = imag = jnp.zeros((16, 128), F32)
            for b in range(2):
                xr, xi = spectra[b, 0, pl.ds(c, 1), :], spectra[b, 1, pl.ds(c, 1), :]
                dr, di = slopes[b, 0], slopes[b, 1]
                real = real + (xr * dr + xi * di)
                imag = imag + (xr * di - xi * dr)
            gm_ref[0, c] = real
            gm_ref[1, c] = imag
            return carry

        lax.fori_loop(0, 16, channel, 0)

    def channel_map(b, k_ref, high_ref, low_ref, target):
        kh, kl = split(k_ref[...])
        for g in range(2):
            cells = slice(g * 16, g * 16 + 16)

            def columns(n, carry):
                cols = pl.ds(pl.multiple_of(n * 256, 256), 256)
                out = dot3(
                    kh,
                    kl,
                    high_ref[b, :, cells, cols].reshape(256, 256),
                    low_ref[b, :, cells, cols].reshape(256, 256),
                )
                target[b, :, cells, cols] = out.reshape(16, 16, 256)
                return carry

            lax.fori_loop(0, 4, columns, 0, unroll=True)

    def slope_stage(ka, b):
        for g in range(2):
            cells = slice(g * 16, g * 16 + 16)
            parts = [ra[ka, b, :, o * 32 + g * 16 : o * 32 + g * 16 + 16, :] for o in range(2)]
            lh, ll = split(jnp.concatenate(parts, axis=1).reshape(256, 256))

            def columns(n, carry):
                cols = pl.ds(pl.multiple_of(n * 256, 256), 256)
                hidden = dot3(lh, ll, th_ref[cols, :], tl_ref[cols, :], (1, 1))
                hidden += field[b, :, cells, cols].reshape(256, 256)
                upstream = gout[b, :, cells, cols].reshape(256, 256) * gelu_slope(hidden)
                high, low = split(upstream)
                fh[b, :, cells, cols] = high.reshape(16, 16, 256)
                fl[b, :, cells, cols] = low.reshape(16, 16, 256)
                return carry

            lax.fori_loop(0, 4, columns, 0, unroll=True)

    small(0).wait()
    small(1).wait()
    build_zt(mz_ref, mt_ref, th_ref, tl_ref)
    store(2).start()
    store(3).start()
    load(0, 0).wait()
    zt_forward(0, 0, fh, fl, field)
    pl.semaphore_wait(barrier, NSX + NSY - 2)
    start_a(0, 0)
    load(1, 0).wait()
    zt_forward(0, 1, fh, fl, field)
    for i in range(2, 6):
        small(i).wait()
    spread_weights(0)
    start_w(0)
    start_a(0, 1)
    build_y(my_ref, ty_ref)
    build_x(mx_ref, tx_ref)
    build_maps(lw_ref, kf_ref, kb_ref)
    build_x_back(mx_ref, txi_ref)
    build_y_back(my_ref, tyi_ref)
    spread_weights(1)

    def map_field(b):
        channel_map(b, kf_ref, fh, fl, field)

    def map_upstream(b):
        channel_map(b, kb_ref, fh, fl, gout)
        store(b).start()

    def there_and_back(k, aside):
        ka = kb = 2 * k
        wait_a(ka, 0)
        y_forward(ka, kb, 0)
        start_b(kb, 0)
        aside(0)
        wait_b(kb, 0)
        x_forward(kb, k, 0)
        if k == 0:
            wait_w(0)
        mix(k, k, 0)
        start_d(k, 0)
        start_c(k, 0)
        wait_a(ka, 1)
        y_forward(ka, kb, 1)
        start_b(kb, 1)
        if k == 0:
            start_w(1)
        wait_d(k, 0)
        x_backward(k, kb + 1, 0)
        start_b(kb + 1, 0)
        wait_b(kb, 1)
        x_forward(kb, k, 1)
        mix(k, k, 1)
        start_d(k, 1)
        start_c(k, 1)
        aside(1)
        wait_d(k, 1)
        x_backward(k, kb + 1, 1)
        start_b(kb + 1, 1)
        wait_b(kb + 1, 0)
        y_backward(kb + 1, ka + 1, 0)
        start_a(ka + 1, 0)
        if k == 1:
            weight_grad()
            store(4).start()
        wait_b(kb + 1, 1)
        y_backward(kb + 1, ka + 1, 1)
        start_a(ka + 1, 1)
        wait_a(ka + 1, 0)

    there_and_back(0, map_field)
    load(0, 1).wait()
    slope_stage(1, 0)
    zt_forward(2, 0, fh, fl)
    start_a(2, 0)
    wait_w(1)
    wait_a(1, 1)
    load(1, 1).wait()
    slope_stage(1, 1)
    zt_forward(2, 1, fh, fl)
    start_a(2, 1)
    there_and_back(1, map_upstream)
    for k in range(2):
        drain(ws.at[k, pl.ds(0, NSY - 1)], None, w_send.at[k])
        for b in range(2):
            drain(sc.at[k, b, pl.ds(0, (NSY - 1) * 8)], None, sc_send.at[k, b])
            drain(sd.at[k, b, pl.ds(0, (NSY - 1) * 32)], None, sd_send.at[k, b])
    for k in range(4):
        for b in range(2):
            drain(sb.at[k, b, pl.ds(0, (NSX - 1) * 8)], None, sb_send.at[k, b])
            drain(sa.at[k, b, pl.ds(0, NSY - 1)], None, sa_send.at[k, b])
    for i in range(5):
        store(i).wait()
    wait_a(3, 1)


def chain(field, gout, weight, local_weight, mode_x, mode_y, mode_z, mode_t):
    shape = jax.ShapeDtypeStruct
    any_space = pl.BlockSpec(memory_space=pl.ANY)
    sems = pltpu.SemaphoreType.DMA
    vmem, smem = pltpu.VMEM, pltpu.SMEM
    return pl.pallas_call(
        chain_kernel,
        out_shape=(
            shape((2, 16, 32, 1024), F32),
            shape((2, 8, 64, 256), F32),
            shape((1024, 256), BF16),
            shape((1024, 256), BF16),
            shape((2, 16, 16, 128), F32),
        ),
        in_specs=[any_space] * 8,
        out_specs=[any_space] * 5,
        scratch_shapes=[
            vmem((2, 16, 32, 1024), F32),
            vmem((2, 16, 32, 1024), F32),
            vmem((2, 16, 32, 1024), BF16),
            vmem((2, 16, 32, 1024), BF16),
            vmem((4, 2, 8, 64, 256), F32),
            vmem((3, 2, 8, 64, 256), F32),
            vmem((4, 2, 256, 128), F32),
            vmem((4, 2, 256, 128), F32),
            vmem((2, 2, 64, 128), F32),
            vmem((2, 2, 64, 128), F32),
            vmem((2, 2, 256, 128), F32),
            vmem((2, 2, 8, 32, 128), F32),
            vmem((2, 8, 2, 2, 16, 128), F32),
            vmem((2, 8, 2, 2, 16, 128), F32),
            vmem((2, 128, 128), F32),
            vmem((2, 2, 16, 128), F32),
            vmem((2, 2, 16, 128), F32),
            vmem((2, 256, 128), F32),
            vmem((16, 16), F32),
            vmem((1024, 256), BF16),
            vmem((1024, 256), BF16),
            vmem((64, 256), F32),
            vmem((256, 32), F32),
            vmem((128, 256), F32),
            vmem((512, 128), F32),
            vmem((256, 256), F32),
            vmem((256, 256), F32),
            vmem((2, 16, 16, 128), F32),
            smem((16,), jnp.int32),
            smem((16,), jnp.int32),
            smem((16,), jnp.int32),
            smem((8,), jnp.int32),
            sems((2, 2)),
            sems((6,)),
            sems((5,)),
        ]
        + [sems((4, 2))] * 6
        + [sems((2, 2))] * 6
        + [sems((2,))] * 3,
        compiler_params=pltpu.CompilerParams(
            collective_id=1, has_side_effects=True, vmem_limit_bytes=56 << 20
        ),
        name="chain",
    )(field, gout, weight, local_weight, mode_x, mode_y, mode_z, mode_t)


def finish_kernel(spectra_ref, local_ref, th_ref, tl_ref, gm_ref, out_ref, gm_out):
    gm_out[...] = gm_ref[...]
    parts = [spectra_ref[0, :, o, :, :] for o in range(2)]
    lh, ll = split(jnp.concatenate(parts, axis=1).reshape(256, 256))

    def columns(n, carry):
        cols = pl.ds(pl.multiple_of(n * 256, 256), 256)
        total = dot3(lh, ll, th_ref[cols, :], tl_ref[cols, :], (1, 1))
        out_ref[0, :, :, cols] = total.reshape(16, 16, 256) + local_ref[0, :, :, cols]
        return carry

    lax.fori_loop(0, 4, columns, 0, unroll=True)


def finish(spectra, local, th, tl, grad_modes):
    cells = pl.BlockSpec((1, 16, 16, 1024), lambda b, g: (b, 0, g, 0))
    table = pl.BlockSpec((1024, 256), lambda b, g: (0, 0))
    modes = pl.BlockSpec((1, 16, 16, 128), lambda b, g: (b, 0, 0, 0))
    return pl.pallas_call(
        finish_kernel,
        grid=(2, 2),
        out_shape=(
            jax.ShapeDtypeStruct((2, 16, 32, 1024), F32),
            jax.ShapeDtypeStruct((2, 16, 16, 128), F32),
        ),
        in_specs=[
            pl.BlockSpec((1, 8, 2, 16, 256), lambda b, g: (b, 0, 0, g, 0)),
            cells,
            table,
            table,
            modes,
        ],
        out_specs=(cells, modes),
        compiler_params=pltpu.CompilerParams(vmem_limit_bytes=60 << 20),
        name="finish",
    )(spectra.reshape(2, 8, 2, 32, 256), local, th, tl, grad_modes)


def body(field, grad_out, local_weight, mode_weight, mode_x, mode_y, mode_z, mode_t):
    local, spectra, th, tl, grad_modes = chain(
        field.reshape(2, 16, 32, 1024),
        grad_out.reshape(2, 16, 32, 1024),
        mode_weight.reshape(2, 256, 128),
        local_weight,
        mode_x,
        mode_y,
        mode_z,
        mode_t,
    )
    grad_input, grad_modes = finish(spectra, local, th, tl, grad_modes)
    return grad_input.reshape(field.shape), grad_modes


def solution(mesh):
    grid = P(None, None, "sx", "sy", None)
    modes = P(None, None, None, ("sx", "sy"))
    return jax.shard_map(
        body,
        mesh=mesh,
        in_specs=(grid, grid, P(), modes, P(), P(), P(), P()),
        out_specs=(grid, modes),
        check_vma=False,
    )
```

```python
import functools
import math

import jax
import jax.numpy as jnp
from jax import lax
from jax.experimental import pallas as pl
from jax.experimental.pallas import tpu as pltpu
from jax.sharding import PartitionSpec as P

MESH = pl.DeviceIdType.MESH
F32 = jnp.float32
BF16 = jnp.bfloat16
NSX = 32
NSY = 8
FORWARD = 1.0 / math.sqrt(128 * 64 * 1024)
INVERSE = 1.0 / math.sqrt(32768)
ROOT_HALF = 1.0 / math.sqrt(2.0)
DENSITY = 1.0 / math.sqrt(2.0 * math.pi)


def iota(shape, dim):
    return lax.broadcasted_iota(jnp.int32, shape, dim)


def split(values):
    high = values.astype(BF16)
    return high, (values - high.astype(F32)).astype(BF16)


def dot(a, b, contract=(1, 0)):
    return lax.dot_general(
        a, b, (((contract[0],), (contract[1],)), ((), ())), preferred_element_type=F32
    )


def dot3(a_high, a_low, b_high, b_low, contract=(1, 0)):
    total = dot(a_high, b_high, contract)
    total += dot(a_high, b_low, contract)
    return total + dot(a_low, b_high, contract)


def mul3(a, b):
    return dot3(*split(a), *split(b))


def turn(phase, length):
    angle = phase.astype(F32) * (2.0 * math.pi / length)
    return jnp.cos(angle), jnp.sin(angle)


def pick(index, mode_ref, count):
    total = jnp.zeros(index.shape, jnp.int32)
    for k in range(count):
        total = jnp.where(index == k, mode_ref[k], total)
    return total


def build_zt(mz_ref, mt_ref, th_ref, tl_ref):
    pair = iota((64, 128), 1)
    cz, sz = turn((iota((64, 128), 0) * pick(pair // 8, mz_ref, 16)) & 63, 64)
    pair = iota((16, 128), 1)
    ct, st = turn((iota((16, 128), 0) * pick(pair % 8, mt_ref, 8)) & 15, 16)
    cz, sz = cz[:, None, :], sz[:, None, :]
    real = (cz * ct - sz * st).reshape(1024, 128)
    imag = (-(sz * ct) - cz * st).reshape(1024, 128)
    th_ref[:, :128], tl_ref[:, :128] = split(real)
    th_ref[:, 128:], tl_ref[:, 128:] = split(imag)


def build_y(my_ref, ty_ref):
    row, col = iota((128, 256), 0), iota((128, 256), 1)
    c, s = turn(((col % 64) * pick(row % 16, my_ref, 16)) & 63, 64)
    same = (row // 64 == col // 128) & ((row // 16) % 2 == (col // 64) % 2)
    ty_ref[...] = jnp.where(same, jnp.where((row // 32) % 2 == 0, c, s), 0.0)


def build_y_back(my_ref, tyi_ref):
    row, col = iota((512, 128), 0), iota((512, 128), 1)
    y = ((row // 32) % 8) * 8 + row % 8
    c, s = turn((y * pick(col % 16, my_ref, 16)) & 63, 64)
    ro, ri = row // 256, (col // 32) % 2
    same = ((row // 8) % 2 == col // 64) & ((row // 16) % 2 == (col // 16) % 2)
    value = jnp.where(ro == ri, c, jnp.where(ro == 0, -s, s))
    tyi_ref[...] = jnp.where(same, value, 0.0)


def build_x(mx_ref, tx_ref):
    row, col = iota((64, 256), 0), iota((64, 256), 1)
    c, s = turn(((col // 2) * pick((row // 8) * 2 + (row // 2) % 2, mx_ref, 16)) & 127, 128)
    ro, ri = row % 2, col % 2
    value = jnp.where(ro == ri, c, jnp.where(ro == 0, s, -s))
    tx_ref[...] = jnp.where(row % 8 < 4, value, 0.0)


def build_x_back(mx_ref, txi_ref):
    row, col = iota((256, 32), 0), iota((256, 32), 1)
    c, s = turn(((row // 2) * pick(col // 2, mx_ref, 16)) & 127, 128)
    ro, ri = row % 2, col % 2
    txi_ref[...] = jnp.where(ro == ri, c, jnp.where(ro == 0, -s, s))


def build_maps(lw_ref, kf_ref, kb_ref):
    row, col = iota((256, 16), 0), iota((256, 16), 1)
    spread = jnp.where(row // 16 == col, 1.0, 0.0)
    high = lax.Precision.HIGHEST
    wide = lax.dot_general(
        spread, lw_ref[...], (((1,), (0,)), ((), ())), precision=high, preferred_element_type=F32
    )
    wide = lax.dot_general(
        wide, spread, (((1,), (1,)), ((), ())), precision=high, preferred_element_type=F32
    )
    row, col = iota((256, 256), 0), iota((256, 256), 1)
    wide = jnp.where(row % 16 == col % 16, wide, 0.0)
    kb_ref[...] = wide
    kf_ref[...] = wide.T


SY_PEERS = ((2, 1), (1, 1), (3, 1), (2, 0), (0, 1), (1, 0), (3, 0))


def swap_lanes(first, second, width):
    low = (iota(first.shape, 1) // width) % 2 == 0
    return (
        jnp.where(low, first, pltpu.roll(second, width, 1)),
        jnp.where(low, pltpu.roll(first, 128 - width, 1), second),
    )


def swap_four(parts):
    a, b, c, d = parts
    a, c = swap_lanes(a, c, 64)
    b, d = swap_lanes(b, d, 64)
    a, b = swap_lanes(a, b, 32)
    c, d = swap_lanes(c, d, 32)
    return a, b, c, d


def gelu_slope(values):
    normal_cdf = 0.5 * (1.0 + lax.erf(values * ROOT_HALF))
    return normal_cdf + values * (jnp.exp(-0.5 * values * values) * DENSITY)


def chain_kernel(
    field_ref, gout_ref, w_hbm, lw_hbm, mx_hbm, my_hbm, mz_hbm, mt_hbm,
    local_out, last_out, th_out, tl_out, gm_out,
    field, gout, fh, fl, sa, ra, sb, rb, sc, rc, sd, rd, ws, wr, turned, spectra, slopes,
    w_ref, lw_ref, th_ref, tl_ref, tx_ref, txi_ref, ty_ref, tyi_ref, kf_ref, kb_ref, gm_ref,
    mx_ref, my_ref, mz_ref, mt_ref,
    load_sem, small_sem, store_sem, sa_send, sa_recv, sa_own, sb_send, sb_recv, sb_own,
    sc_send, sc_recv, sc_own, sd_send, sd_recv, sd_own, w_send, w_recv, w_own,
):
    sx, sy = lax.axis_index("sx"), lax.axis_index("sy")

    def load(b, which):
        source, target = ((field_ref, field), (gout_ref, gout))[which]
        return pltpu.make_async_copy(source.at[b], target.at[b], load_sem.at[which, b])

    def small(i):
        source = (mz_hbm, mt_hbm, mx_hbm, my_hbm, lw_hbm, w_hbm)[i]
        target = (mz_ref, mt_ref, mx_ref, my_ref, lw_ref, w_ref)[i]
        return pltpu.make_async_copy(source, target, small_sem.at[i])

    def store(i):
        source = (gout.at[0], gout.at[1], th_ref, tl_ref, gm_ref)[i]
        target = (local_out.at[0], local_out.at[1], th_out, tl_out, gm_out)[i]
        return pltpu.make_async_copy(source, target, store_sem.at[i])

    small(0).start()
    small(1).start()
    load(0, 0).start()
    barrier = pltpu.get_barrier_semaphore()

    def greet(axis, me, n):
        def one(d, carry):
            pl.semaphore_signal(
                barrier, inc=1, device_id={axis: lax.rem(me + d, n)}, device_id_type=MESH
            )
            return carry

        lax.fori_loop(1, n, one, 0)

    greet("sy", sy, NSY)
    greet("sx", sx, NSX)
    for i in range(2, 6):
        small(i).start()
    load(1, 0).start()
    load(0, 1).start()
    load(1, 1).start()

    def send(axis, to, source, target, sems):
        pltpu.make_async_remote_copy(
            src_ref=source,
            dst_ref=target,
            send_sem=sems[0],
            recv_sem=sems[1],
            device_id={axis: to},
            device_id_type=MESH,
        ).start()

    def over_sy(source, target, sems):
        for dy, dx in SY_PEERS:
            to = lax.rem(sy // 2 + dy, 4) * 2 + lax.rem(sy + dx, 2)
            send("sy", to, source(to), target(sy), sems)
        pltpu.make_async_copy(source(sy), target(sy), sems[2]).start()

    def over_sx(source, target, sems):
        def at(dx, dz, dc):
            to = lax.rem(sx // 16 + dx, 2) * 16 + lax.rem(sx // 2 + dz, 8) * 2 + lax.rem(sx + dc, 2)
            send("sx", to, source(to), target(sx), sems)

        def ring(j, carry):
            dz = 12 + ((j + 1) // 2) * (2 * lax.rem(j, 2) - 1)
            for dx, dc in ((1, 1), (1, 0), (0, 1), (0, 0)):
                at(dx, dz, dc)
            return carry

        lax.fori_loop(0, 7, ring, 0)
        for dx, dc in ((1, 1), (1, 0), (0, 1)):
            at(dx, 0, dc)
        pltpu.make_async_copy(source(sx), target(sx), sems[2]).start()

    def drain(whole, one, sem, own=None):
        pltpu.make_async_copy(whole, whole, sem).wait()
        if own is not None:
            pltpu.make_async_copy(one, one, own).wait()

    def eight(d):
        return pl.ds(pl.multiple_of(d * 8, 8), 8)

    def start_a(k, b):
        target = (lambda d: ra.at[k, b, d]) if k < 3 else (lambda d: last_out.at[b, d])
        over_sy(lambda d: sa.at[k, b, d], target, (sa_send.at[k, b], sa_recv.at[k, b], sa_own.at[k, b]))

    def wait_a(k, b):
        whole = ra.at[k, b] if k < 3 else last_out.at[b]
        drain(whole.at[pl.ds(0, NSY - 1)], whole.at[0], sa_recv.at[k, b], sa_own.at[k, b])

    def start_b(k, b):
        over_sx(
            lambda d: sb.at[k, b, eight(d)],
            lambda d: rb.at[k, b, eight(d)],
            (sb_send.at[k, b], sb_recv.at[k, b], sb_own.at[k, b]),
        )

    def wait_b(k, b):
        whole = rb.at[k, b]
        drain(whole.at[pl.ds(0, (NSX - 1) * 8)], whole.at[pl.ds(0, 8)], sb_recv.at[k, b], sb_own.at[k, b])

    def start_c(k, b):
        over_sy(
            lambda d: sc.at[k, b, eight(d)],
            lambda d: rc.at[k, b, eight(d)],
            (sc_send.at[k, b], sc_recv.at[k, b], sc_own.at[k, b]),
        )

    def wait_c(k, b):
        whole = rc.at[k, b]
        drain(whole.at[pl.ds(0, (NSY - 1) * 8)], whole.at[pl.ds(0, 8)], sc_recv.at[k, b], sc_own.at[k, b])

    def start_d(k, b):
        over_sy(
            lambda d: sd.at[k, b, pl.ds(pl.multiple_of(d * 32, 32), 32)],
            lambda d: rd.at[k, b, d],
            (sd_send.at[k, b], sd_recv.at[k, b], sd_own.at[k, b]),
        )

    def wait_d(k, b):
        whole = rd.at[k, b]
        drain(whole.at[pl.ds(0, NSY - 1)], whole.at[0], sd_recv.at[k, b], sd_own.at[k, b])

    def start_w(k):
        over_sy(lambda d: ws.at[k, d], lambda d: wr.at[k, d], (w_send.at[k], w_recv.at[k], w_own.at[k]))

    def wait_w(k):
        whole = wr.at[k]
        drain(whole.at[pl.ds(0, NSY - 1)], whole.at[0], w_recv.at[k], w_own.at[k])

    def zt_forward(k, b, high_ref, low_ref, source=None):
        def block(m, carry):
            rows = pl.ds(m * 8, 8)
            if source is None:
                high = high_ref[b, rows].reshape(256, 1024)
                low = low_ref[b, rows].reshape(256, 1024)
            else:
                high, low = split(source[b, rows].reshape(256, 1024))
                high_ref[b, rows] = high.reshape(8, 32, 1024)
                low_ref[b, rows] = low.reshape(8, 32, 1024)
            out = dot3(high, low, th_ref[...], tl_ref[...])
            sa[k, b, pl.ds(m * 4, 4)] = out.reshape(4, 64, 256)
            return carry

        lax.fori_loop(0, 2, block, 0)

    def y_forward(ka, kb, b):
        for i in range(2):
            parts = [
                ra[ka, b, :, c * 32 + (i * 2 + x) * 8 : c * 32 + (i * 2 + x) * 8 + 8, :].reshape(64, 256)
                for x in range(2)
                for c in range(2)
            ]
            out = mul3(ty_ref[...], jnp.concatenate(parts, axis=0))
            rows = []
            for x in range(2):
                cos, sin = out[x * 64 : x * 64 + 32], out[x * 64 + 32 : x * 64 + 64]
                rows.append(cos[:, :128] + sin[:, 128:])
                rows.append(cos[:, 128:] - sin[:, :128])
            turned[i] = jnp.concatenate(rows, axis=0).T
            parts = swap_four([turned[i, pl.ds(z, 32, stride=4), :] for z in range(4)])
            for q in range(4):
                sb[kb, b, pl.ds(i * 4 + q, 32, stride=8), :] = parts[q]

    def y_backward(kb, ka, b):
        halves = []
        for i in range(2):
            parts = swap_four([rb[kb, b, pl.ds(i * 4 + q, 32, stride=8), :] for q in range(4)])
            for z in range(4):
                turned[i, pl.ds(z, 32, stride=4), :] = parts[z]
            halves.append(turned[i].T)
        out = mul3(tyi_ref[...], jnp.concatenate(halves, axis=1))
        for part in range(2):
            for i in range(2):
                block = out[part * 256 : part * 256 + 256, i * 128 : i * 128 + 128].reshape(8, 2, 16, 128)
                for o in range(2):
                    sa[ka, b, :, o * 32 + i * 16 : o * 32 + i * 16 + 16, part * 128 : part * 128 + 128] = block[:, o]

    def x_forward(kb, kc, b):
        sc[kc, b] = mul3(tx_ref[...], rb[kb, b])

    def x_backward(kd, kb, b):
        total = rd[kd, b, 0]
        for d in range(1, NSY):
            total += rd[kd, b, d]
        sb[kb, b] = mul3(txi_ref[...], total * (FORWARD * INVERSE))

    def gather_modes(kc, b, keep, factor):
        for part in range(2):
            pair = swap_lanes(
                rc[kc, b, pl.ds(part, 8, stride=8), :], rc[kc, b, pl.ds(2 + part, 8, stride=8), :], 16
            )
            for low in range(2):
                keep[b, part, pl.ds(low, 8, stride=2), :] = pair[low] * factor

    def spread_weights(k):
        inner, outer = (1, 16) if k == 0 else (16, 1)
        for part in range(2):
            for slab in range(NSY):
                for low in range(2):
                    pair = [
                        w_ref[part, pl.ds((slab * 2 + own) * outer + low * inner, 8, stride=2 * inner), :]
                        for own in range(2)
                    ]
                    pair = swap_lanes(pair[0], pair[1], 16)
                    for kx in range(2):
                        ws[k, slab, part, kx, low * 8 : low * 8 + 8, :] = pair[kx]

    def mix(kc, kd, b):
        sign = 1.0 if kd == 0 else -1.0
        low = (iota((8, 128), 1) // 16) % 2 == 0

        def fold(values):
            even, odd = values[:8], values[8:]
            return jnp.where(low, even + pltpu.roll(even, 112, 1), odd + pltpu.roll(odd, 16, 1))

        def line(i, carry):
            for kx in range(2):
                real = sc[kc, b, pl.ds(i * 8 + kx * 2, 1), :]
                imag = sc[kc, b, pl.ds(i * 8 + kx * 2 + 1, 1), :]
                w_real, w_imag = wr[kd, i, 0, kx], wr[kd, i, 1, kx]
                out_real = w_real * real - sign * (w_imag * imag)
                out_imag = w_real * imag + sign * (w_imag * real)
                sd[kd, b, pl.ds(i * 4 + kx * 2, 8, stride=32), :] = fold(out_real)
                sd[kd, b, pl.ds(i * 4 + kx * 2 + 1, 8, stride=32), :] = fold(out_imag)
            return carry

        lax.fori_loop(0, NSY, line, 0, unroll=True)

    def weight_grad():
        for b in range(2):
            wait_c(0, b)
            gather_modes(0, b, spectra, FORWARD)
            wait_c(1, b)
            gather_modes(1, b, slopes, INVERSE)

        def channel(c, carry):
            real = imag = jnp.zeros((16, 128), F32)
            for b in range(2):
                xr, xi = spectra[b, 0, pl.ds(c, 1), :], spectra[b, 1, pl.ds(c, 1), :]
                dr, di = slopes[b, 0], slopes[b, 1]
                real = real + (xr * dr + xi * di)
                imag = imag + (xr * di - xi * dr)
            gm_ref[0, c] = real
            gm_ref[1, c] = imag
            return carry

        lax.fori_loop(0, 16, channel, 0)

    def channel_map(b, k_ref, high_ref, low_ref, target):
        kh, kl = split(k_ref[...])
        for g in range(2):
            cells = slice(g * 16, g * 16 + 16)

            def columns(n, carry):
                cols = pl.ds(pl.multiple_of(n * 256, 256), 256)
                out = dot3(
                    kh,
                    kl,
                    high_ref[b, :, cells, cols].reshape(256, 256),
                    low_ref[b, :, cells, cols].reshape(256, 256),
                )
                target[b, :, cells, cols] = out.reshape(16, 16, 256)
                return carry

            lax.fori_loop(0, 4, columns, 0, unroll=True)

    def slope_stage(ka, b):
        for g in range(2):
            cells = slice(g * 16, g * 16 + 16)
            parts = [ra[ka, b, :, o * 32 + g * 16 : o * 32 + g * 16 + 16, :] for o in range(2)]
            lh, ll = split(jnp.concatenate(parts, axis=1).reshape(256, 256))

            def columns(n, carry):
                cols = pl.ds(pl.multiple_of(n * 256, 256), 256)
                hidden = dot3(lh, ll, th_ref[cols, :], tl_ref[cols, :], (1, 1))
                hidden += field[b, :, cells, cols].reshape(256, 256)
                upstream = gout[b, :, cells, cols].reshape(256, 256) * gelu_slope(hidden)
                high, low = split(upstream)
                fh[b, :, cells, cols] = high.reshape(16, 16, 256)
                fl[b, :, cells, cols] = low.reshape(16, 16, 256)
                return carry

            lax.fori_loop(0, 4, columns, 0, unroll=True)

    small(0).wait()
    small(1).wait()
    build_zt(mz_ref, mt_ref, th_ref, tl_ref)
    store(2).start()
    store(3).start()
    load(0, 0).wait()
    zt_forward(0, 0, fh, fl, field)
    pl.semaphore_wait(barrier, NSX + NSY - 2)
    start_a(0, 0)
    load(1, 0).wait()
    zt_forward(0, 1, fh, fl, field)
    for i in range(2, 6):
        small(i).wait()
    spread_weights(0)
    start_w(0)
    start_a(0, 1)
    build_y(my_ref, ty_ref)
    build_x(mx_ref, tx_ref)
    build_maps(lw_ref, kf_ref, kb_ref)
    build_x_back(mx_ref, txi_ref)
    build_y_back(my_ref, tyi_ref)
    spread_weights(1)

    def map_field(b):
        channel_map(b, kf_ref, fh, fl, field)

    def map_upstream(b):
        channel_map(b, kb_ref, fh, fl, gout)
        store(b).start()

    def there_and_back(k, aside):
        ka = kb = 2 * k
        wait_a(ka, 0)
        y_forward(ka, kb, 0)
        start_b(kb, 0)
        aside(0)
        wait_b(kb, 0)
        x_forward(kb, k, 0)
        if k == 0:
            wait_w(0)
        mix(k, k, 0)
        start_d(k, 0)
        start_c(k, 0)
        wait_a(ka, 1)
        y_forward(ka, kb, 1)
        start_b(kb, 1)
        if k == 0:
            start_w(1)
        wait_d(k, 0)
        x_backward(k, kb + 1, 0)
        start_b(kb + 1, 0)
        wait_b(kb, 1)
        x_forward(kb, k, 1)
        mix(k, k, 1)
        start_d(k, 1)
        start_c(k, 1)
        aside(1)
        wait_d(k, 1)
        x_backward(k, kb + 1, 1)
        start_b(kb + 1, 1)
        wait_b(kb + 1, 0)
        y_backward(kb + 1, ka + 1, 0)
        start_a(ka + 1, 0)
        if k == 1:
            weight_grad()
            store(4).start()
        wait_b(kb + 1, 1)
        y_backward(kb + 1, ka + 1, 1)
        start_a(ka + 1, 1)
        wait_a(ka + 1, 0)

    there_and_back(0, map_field)
    load(0, 1).wait()
    slope_stage(1, 0)
    zt_forward(2, 0, fh, fl)
    start_a(2, 0)
    wait_w(1)
    wait_a(1, 1)
    load(1, 1).wait()
    slope_stage(1, 1)
    zt_forward(2, 1, fh, fl)
    start_a(2, 1)
    there_and_back(1, map_upstream)
    for k in range(2):
        drain(ws.at[k, pl.ds(0, NSY - 1)], None, w_send.at[k])
        for b in range(2):
            drain(sc.at[k, b, pl.ds(0, (NSY - 1) * 8)], None, sc_send.at[k, b])
            drain(sd.at[k, b, pl.ds(0, (NSY - 1) * 32)], None, sd_send.at[k, b])
    for k in range(4):
        for b in range(2):
            drain(sb.at[k, b, pl.ds(0, (NSX - 1) * 8)], None, sb_send.at[k, b])
            drain(sa.at[k, b, pl.ds(0, NSY - 1)], None, sa_send.at[k, b])
    for i in range(5):
        store(i).wait()
    wait_a(3, 1)


def chain(field, gout, weight, local_weight, mode_x, mode_y, mode_z, mode_t):
    shape = jax.ShapeDtypeStruct
    any_space = pl.BlockSpec(memory_space=pl.ANY)
    sems = pltpu.SemaphoreType.DMA
    vmem, smem = pltpu.VMEM, pltpu.SMEM
    return pl.pallas_call(
        chain_kernel,
        out_shape=(
            shape((2, 16, 32, 1024), F32),
            shape((2, 8, 64, 256), F32),
            shape((1024, 256), BF16),
            shape((1024, 256), BF16),
            shape((2, 16, 16, 128), F32),
        ),
        in_specs=[any_space] * 8,
        out_specs=[any_space] * 5,
        scratch_shapes=[
            vmem((2, 16, 32, 1024), F32),
            vmem((2, 16, 32, 1024), F32),
            vmem((2, 16, 32, 1024), BF16),
            vmem((2, 16, 32, 1024), BF16),
            vmem((4, 2, 8, 64, 256), F32),
            vmem((3, 2, 8, 64, 256), F32),
            vmem((4, 2, 256, 128), F32),
            vmem((4, 2, 256, 128), F32),
            vmem((2, 2, 64, 128), F32),
            vmem((2, 2, 64, 128), F32),
            vmem((2, 2, 256, 128), F32),
            vmem((2, 2, 8, 32, 128), F32),
            vmem((2, 8, 2, 2, 16, 128), F32),
            vmem((2, 8, 2, 2, 16, 128), F32),
            vmem((2, 128, 128), F32),
            vmem((2, 2, 16, 128), F32),
            vmem((2, 2, 16, 128), F32),
            vmem((2, 256, 128), F32),
            vmem((16, 16), F32),
            vmem((1024, 256), BF16),
            vmem((1024, 256), BF16),
            vmem((64, 256), F32),
            vmem((256, 32), F32),
            vmem((128, 256), F32),
            vmem((512, 128), F32),
            vmem((256, 256), F32),
            vmem((256, 256), F32),
            vmem((2, 16, 16, 128), F32),
            smem((16,), jnp.int32),
            smem((16,), jnp.int32),
            smem((16,), jnp.int32),
            smem((8,), jnp.int32),
            sems((2, 2)),
            sems((6,)),
            sems((5,)),
        ]
        + [sems((4, 2))] * 6
        + [sems((2, 2))] * 6
        + [sems((2,))] * 3,
        compiler_params=pltpu.CompilerParams(
            collective_id=1, has_side_effects=True, vmem_limit_bytes=56 << 20
        ),
        name="chain",
    )(field, gout, weight, local_weight, mode_x, mode_y, mode_z, mode_t)


def finish_kernel(
    spectra_hbm, local_hbm, th_hbm, tl_hbm, gm_hbm, out_hbm, gm_out, spectra, local, th, tl, gm, load_sem, store_sem
):
    def load(i):
        source = (th_hbm, tl_hbm, spectra_hbm.at[0], spectra_hbm.at[1], gm_hbm)[i]
        target = (th, tl, spectra.at[0], spectra.at[1], gm)[i]
        return pltpu.make_async_copy(source, target, load_sem.at[i])

    def part(hbm, b, g, sem, out):
        rows = (b, slice(None), pl.ds(g * 16, 16))
        pair = (local.at[rows], hbm.at[rows]) if out else (hbm.at[rows], local.at[rows])
        return pltpu.make_async_copy(*pair, sem)

    order = [(b, g) for b in range(2) for g in range(2)]
    for i in range(3):
        load(i).start()
    for i, (b, g) in enumerate(order):
        part(local_hbm, b, g, load_sem.at[5 + i], False).start()
        if i == 0:
            load(3).start()
    load(4).start()
    load(0).wait()
    load(1).wait()
    for i, (b, g) in enumerate(order):
        if g == 0:
            load(2 + b).wait()
        lh, ll = split(jnp.concatenate([spectra[b, :, o, g * 16 : g * 16 + 16, :] for o in range(2)], axis=1).reshape(256, 256))
        part(local_hbm, b, g, load_sem.at[5 + i], False).wait()
        cells = slice(g * 16, g * 16 + 16)
        for n in range(4):
            cols = slice(n * 256, n * 256 + 256)
            total = dot3(lh, ll, th[cols, :], tl[cols, :], (1, 1))
            local[b, :, cells, cols] = total.reshape(16, 16, 256) + local[b, :, cells, cols]
        part(out_hbm, b, g, store_sem.at[i], True).start()
        if i == 0:
            load(4).wait()
            pltpu.make_async_copy(gm, gm_out, store_sem.at[4]).start()
    for i, (b, g) in enumerate(order):
        part(out_hbm, b, g, store_sem.at[i], True).wait()
    pltpu.make_async_copy(gm, gm_out, store_sem.at[4]).wait()


def finish(spectra, local, th, tl, grad_modes):
    any_space = pl.BlockSpec(memory_space=pl.ANY)
    vmem = pltpu.VMEM
    return pl.pallas_call(
        finish_kernel,
        out_shape=(
            jax.ShapeDtypeStruct((2, 16, 32, 1024), F32),
            jax.ShapeDtypeStruct((2, 16, 16, 128), F32),
        ),
        in_specs=[any_space] * 5,
        out_specs=(any_space, any_space),
        scratch_shapes=[
            vmem((2, 8, 2, 32, 256), F32),
            vmem((2, 16, 32, 1024), F32),
            vmem((1024, 256), BF16),
            vmem((1024, 256), BF16),
            vmem((2, 16, 16, 128), F32),
            pltpu.SemaphoreType.DMA((9,)),
            pltpu.SemaphoreType.DMA((5,)),
        ],
        compiler_params=pltpu.CompilerParams(vmem_limit_bytes=60 << 20),
        name="finish",
    )(spectra.reshape(2, 8, 2, 32, 256), local, th, tl, grad_modes)


def body(field, grad_out, local_weight, mode_weight, mode_x, mode_y, mode_z, mode_t):
    local, spectra, th, tl, grad_modes = chain(
        field.reshape(2, 16, 32, 1024),
        grad_out.reshape(2, 16, 32, 1024),
        mode_weight.reshape(2, 256, 128),
        local_weight,
        mode_x,
        mode_y,
        mode_z,
        mode_t,
    )
    grad_input, grad_modes = finish(spectra, local, th, tl, grad_modes)
    return grad_input.reshape(field.shape), grad_modes


def solution(mesh):
    grid = P(None, None, "sx", "sy", None)
    modes = P(None, None, None, ("sx", "sy"))
    return jax.shard_map(
        body,
        mesh=mesh,
        in_specs=(grid, grid, P(), modes, P(), P(), P(), P()),
        out_specs=(grid, modes),
        check_vma=False,
    )
```
